32 devices in a mesh: groups: 2 (over y), tensor: 8 (over z, x), dp: 2 (over core).
Axes of the slice: x: 2, y: 2, z: 4, core: 2. Of those that a mesh axis runs over, the one named last changes fastest.
Arguments:
- gate_pre: bfloat16 [2048, 28672], P(('groups', 'dp'), 'tensor'), parts along dimension 0, may hold values from -6 to 6
- up_pre: bfloat16 [2048, 28672], P(('groups', 'dp'), 'tensor'), parts along dimension 0, may hold values from -16 to 16
- down_weight: bfloat16 [28672, 4096], P('tensor'), may hold values from -0.375 to 0.375
- out_grad: bfloat16 [2048, 4096], P(('groups', 'dp'), 'tensor'), parts along dimension 0, may hold values from -2.5 to 2.5
Outputs:
- grad_gate: bfloat16 [2048, 28672], P(('groups', 'dp'), 'tensor'), parts along dimension 0
- grad_up: bfloat16 [2048, 28672], P(('groups', 'dp'), 'tensor'), parts along dimension 0
- grad_down: bfloat16 [57344, 4096], P(('groups', 'tensor'), 'dp'), parts along dimension 0
The draws below stay inside these ranges and needn't reach their ends.
There are 2 independent parts, one for each index of `groups`. The reference program is written for one: setup_inputs(seed, part) draws one part's arguments, and reference() takes and returns one part's arrays. A program takes and returns all parts, laid end to end along the dimension named above; an argument that names none is the same for every part. Nothing has to cross between parts.
All inputs are finite; a program needn't handle non-finite values.
Results may differ from the reference program's by a relative error of at most 0.0061.
Values may be sent and summed in bfloat16 or wider, within the bound.
A program may use at most 320 MiB of HBM per device.

```python
import math
import jax
import jax.numpy as jnp
import numpy as np
from jax import lax

D = 4096
HAD_LARGE = 1024
GROUP = 128
FF = 28672
TOKENS = 1024


def draw_up_pre(key, part):
    key = jax.random.fold_in(key, 5)
    row_key, entry_key = jax.random.split(key, 2)
    row_scale = jnp.exp(jax.random.uniform(row_key, (TOKENS, 1), jnp.float32, math.log(0.4), math.log(4.0)))
    entries = jnp.clip(jax.random.normal(entry_key, (TOKENS, FF), jnp.float32), -4.0, 4.0)
    return (row_scale * entries).astype(jnp.bfloat16)


def block_levels(own_key, dims, cuts, smallest, top_value):
    gain, own = 1.0, jax.random.fold_in(own_key, 6)
    for axis_at, shards_of in cuts:
        heights = jnp.exp(jax.random.uniform(jax.random.fold_in(own, axis_at), (shards_of,), jnp.float32, smallest / len(cuts), top_value / len(cuts)))
        gain = gain * jnp.repeat(heights, dims[axis_at] // shards_of).reshape([-1 if axis == axis_at else 1 for axis in range(len(dims))])
    return gain


def bell_draw(own_key, extent, scale, reach, cuts=(), kind=jnp.bfloat16):
    factor_of = block_levels(own_key, extent, cuts, -0.22, 0.18) if cuts else 1.0
    values = jax.random.normal(own_key, extent, jnp.float32) * scale * factor_of
    return jnp.minimum(jnp.maximum(values, -reach), reach).astype(kind)


def setup_inputs(seed: int = 0, part: int = 0) -> dict:
    seeds = jax.random.split(jax.random.key(seed), 5)
    own_keys = jax.random.split(jax.random.fold_in(seeds[4], part), 5)
    gate_pre = bell_draw(own_keys[0], (TOKENS, FF), 1.0, 6.0, ((0, 2), (1, 8)))
    up_pre = draw_up_pre(jax.random.fold_in(jax.random.fold_in(seeds[4], part), 71), part)
    down_weight = bell_draw(seeds[2], (FF, D), (D // 16) ** -0.5, 0.375, ((0, 8),))
    out_grad = bell_draw(own_keys[3], (TOKENS, D), 0.25, 2.5, ((0, 2), (1, 8)))
    return dict(gate_pre=gate_pre, up_pre=up_pre, down_weight=down_weight, out_grad=out_grad)


def paley_table():
    residues = set((number * number % 13 for number in range(1, 13)))
    core_matrix = np.zeros((14, 14))
    core_matrix[0, 1:] = 1.0
    core_matrix[1:, 0] = 1.0
    for row_index in range(13):
        for col_index in range(13):
            offset = (col_index - row_index) % 13
            if offset != 0:
                core_matrix[row_index + 1, col_index + 1] = 1.0 if offset in residues else -1.0
    upper_block = np.array([[1.0, 1.0], [1.0, -1.0]])
    diagonal_block = np.array([[1.0, -1.0], [-1.0, -1.0]])
    return np.kron(core_matrix, upper_block) + np.kron(np.eye(14), diagonal_block)

def sylvester(matrix_order):
    positions = jnp.arange(matrix_order, dtype=jnp.int32)
    common_bits = jnp.bitwise_and(positions[:, None], positions[None, :])
    parity = jnp.zeros((matrix_order, matrix_order), jnp.int32)
    for bit_shift in range(matrix_order.bit_length() - 1):
        parity = parity + jnp.bitwise_and(jnp.right_shift(common_bits, bit_shift), 1)
    return (1 - 2 * (parity % 2)).astype(jnp.float32)

def rotate(rows_in, small_table, large_table):
    row_count, width = rows_in.shape
    large_order = large_table.shape[0]
    small_order = small_table.shape[0]
    first_section = jnp.dot(rows_in.reshape(row_count * small_order, large_order), large_table, preferred_element_type=jnp.float32)
    first_section = first_section.reshape(row_count, small_order, large_order)
    rotated = jnp.einsum('ac,tad->tcd', small_table, first_section, precision=lax.Precision.HIGHEST)
    return rotated.reshape(row_count, width) * (1.0 / math.sqrt(width))

def quantize(rotated):
    grouped = rotated.reshape(rotated.shape[0], -1, GROUP)
    largest = lax.optimization_barrier(jnp.max(jnp.abs(grouped), axis=-1, keepdims=True))
    spacing = largest * (0.9 / 7.0) + 1e-06
    scaled = grouped / spacing
    staircase = jnp.minimum(scaled - jnp.sin(2.0 * math.pi * scaled) / (2.0 * math.pi), 7.0)
    return (staircase * spacing).reshape(rotated.shape).astype(jnp.bfloat16)

def reference(gate_pre, up_pre, down_weight, out_grad):
    small_table = jnp.asarray(paley_table(), jnp.float32)
    large_table = sylvester(HAD_LARGE).astype(jnp.bfloat16)
    gate_wide = gate_pre.astype(jnp.float32)
    up_wide = up_pre.astype(jnp.float32)
    sigmoid_gate = jax.nn.sigmoid(gate_wide)
    activated = gate_wide * sigmoid_gate
    hidden = (activated * up_wide).astype(jnp.bfloat16)
    quantized = quantize(rotate(hidden, small_table, large_table))
    grad_down = jnp.dot(quantized.T, out_grad, preferred_element_type=jnp.float32).astype(jnp.bfloat16)
    rot_grad = jnp.dot(out_grad, down_weight.T, preferred_element_type=jnp.float32).astype(jnp.bfloat16)
    hidden_grad = rotate(rot_grad, small_table.T, large_table.T).astype(jnp.bfloat16)
    hid_wide = hidden_grad.astype(jnp.float32)
    grad_up = (hid_wide * activated).astype(jnp.bfloat16)
    grad_gate = (hid_wide * up_wide * sigmoid_gate * (1.0 + gate_wide * (1.0 - sigmoid_gate))).astype(jnp.bfloat16)
    return (grad_gate, grad_up, grad_down)
```

```python
import functools
import math

import jax
import jax.numpy as jnp
import numpy as np
from jax import lax
from jax.experimental import pallas as pl
from jax.experimental.pallas import tpu as pltpu
from jax.sharding import PartitionSpec as P

HAD_LARGE = 1024
GROUP = 128
PIECE = 512
MESH = pl.DeviceIdType.MESH
ANY = pl.BlockSpec(memory_space=pl.ANY)
VMEM_LIMIT = 56 * 1024 * 1024


def paley_table():
    residues = set((number * number % 13 for number in range(1, 13)))
    core_matrix = np.zeros((14, 14))
    core_matrix[0, 1:] = 1.0
    core_matrix[1:, 0] = 1.0
    for row_index in range(13):
        for col_index in range(13):
            offset = (col_index - row_index) % 13
            if offset != 0:
                core_matrix[row_index + 1, col_index + 1] = 1.0 if offset in residues else -1.0
    upper_block = np.array([[1.0, 1.0], [1.0, -1.0]])
    diagonal_block = np.array([[1.0, -1.0], [-1.0, -1.0]])
    return np.kron(core_matrix, upper_block) + np.kron(np.eye(14), diagonal_block)


def sylvester(matrix_order):
    positions = jnp.arange(matrix_order, dtype=jnp.int32)
    common_bits = jnp.bitwise_and(positions[:, None], positions[None, :])
    parity = jnp.zeros((matrix_order, matrix_order), jnp.int32)
    for bit_shift in range(matrix_order.bit_length() - 1):
        parity = parity + jnp.bitwise_and(jnp.right_shift(common_bits, bit_shift), 1)
    return (1 - 2 * (parity % 2)).astype(jnp.float32)


def rotate(rows_in, small_table, large_table):
    row_count, width = rows_in.shape
    large_order = large_table.shape[0]
    small_order = small_table.shape[0]
    first_section = jnp.dot(
        rows_in.reshape(row_count * small_order, large_order),
        large_table,
        preferred_element_type=jnp.float32,
    )
    first_section = first_section.reshape(row_count, small_order, large_order)
    rotated = jnp.einsum("ac,tad->tcd", small_table, first_section, precision=lax.Precision.HIGHEST)
    return rotated.reshape(row_count, width) * (1.0 / math.sqrt(width))


def quantize(rotated):
    grouped = rotated.reshape(rotated.shape[0], -1, GROUP)
    largest = jnp.max(jnp.abs(grouped), axis=-1, keepdims=True)
    spacing = largest * (0.9 / 7.0) + 1e-06
    scaled = grouped / spacing
    staircase = jnp.minimum(scaled - jnp.sin(2.0 * math.pi * scaled) / (2.0 * math.pi), 7.0)
    return (staircase * spacing).reshape(rotated.shape).astype(jnp.bfloat16)


def per_device(gate_pre, up_pre, down_weight, out_grad):
    small_table = jnp.asarray(paley_table(), jnp.float32)
    large_table = sylvester(HAD_LARGE).astype(jnp.bfloat16)
    gate_wide = gate_pre.astype(jnp.float32)
    up_wide = up_pre.astype(jnp.float32)
    sigmoid_gate = jax.nn.sigmoid(gate_wide)
    activated = gate_wide * sigmoid_gate
    hidden = (activated * up_wide).astype(jnp.bfloat16)
    full_grad = lax.all_gather(out_grad, "tensor", axis=1, tiled=True)
    rot_grad = lax.dot_general(
        full_grad, down_weight, (((1,), (1,)), ((), ())), preferred_element_type=jnp.float32
    ).astype(jnp.bfloat16)
    token_hidden = lax.all_to_all(hidden, "tensor", split_axis=0, concat_axis=1, tiled=True)
    quant_rows = quantize(rotate(token_hidden, small_table, large_table))
    quantized = lax.all_to_all(quant_rows, "tensor", split_axis=1, concat_axis=0, tiled=True)
    token_grad = lax.all_to_all(rot_grad, "tensor", split_axis=0, concat_axis=1, tiled=True)
    back_rows = rotate(token_grad, small_table.T, large_table.T).astype(jnp.bfloat16)
    hidden_grad = lax.all_to_all(back_rows, "tensor", split_axis=1, concat_axis=0, tiled=True)
    partial_grad = lax.dot_general(
        quantized, full_grad, (((0,), (0,)), ((), ())), preferred_element_type=jnp.float32
    )
    grad_down = lax.psum_scatter(partial_grad, "dp", scatter_dimension=1, tiled=True).astype(
        jnp.bfloat16
    )
    hid_wide = hidden_grad.astype(jnp.float32)
    grad_up = (hid_wide * activated).astype(jnp.bfloat16)
    grad_gate = (
        hid_wide * up_wide * sigmoid_gate * (1.0 + gate_wide * (1.0 - sigmoid_gate))
    ).astype(jnp.bfloat16)
    return (grad_gate, grad_up, grad_down)


def conference():
    signs = paley_table()[::2, ::2].copy()
    np.fill_diagonal(signs, 0.0)
    return signs


SINE = tuple((0.9999999944722885, -6.579735439437039, 12.987842893122675, -12.207428862951517, 6.6870661467168215, -2.3663670610371574, 0.5091905912043592))


def greet(n, sibling=False):
    me = lax.axis_index("tensor")
    barrier = pltpu.get_barrier_semaphore()
    for step in range(1, n):
        pl.semaphore_signal(
            barrier, inc=1, device_id={"tensor": lax.rem(me + step, n)}, device_id_type=MESH
        )
    if sibling:
        other = 1 - lax.axis_index("dp")
        pl.semaphore_signal(barrier, inc=1, device_id={"dp": other}, device_id_type=MESH)
    pl.semaphore_wait(barrier, n if sibling else n - 1)


def start_exchange(n, source, target, send, recv, own):
    me = lax.axis_index("tensor")
    pending = []
    for step in sorted(range(1, n), key=lambda s: abs(s - n // 2)):
        peer = lax.rem(me + step, n)
        copy = pltpu.make_async_remote_copy(
            src_ref=source.at[peer],
            dst_ref=target.at[me],
            send_sem=send.at[step],
            recv_sem=recv.at[step],
            device_id={"tensor": peer},
            device_id_type=MESH,
        )
        copy.start()
        pending.append(copy)
    local = pltpu.make_async_copy(source.at[me], target.at[me], own)
    local.start()
    pending.append(local)
    return pending


def forward_kernel(
    n, hidden, out_grad, weight, full_grad, token_hidden, rot_grad,
    weight_v, grad_v, rot_v, send, recv, own, gather_send, gather_recv, local_sem, weight_sem,
):
    me = lax.axis_index("tensor")
    pairs = n // 2
    row, side = me // 2, lax.rem(me, 2)
    width = out_grad.shape[1]
    load_weight = pltpu.make_async_copy(weight, weight_v, weight_sem)
    load_weight.start()
    greet(n)
    partner = row * 2 + 1 - side

    def push(source, slot, peer, at):
        return pltpu.make_async_remote_copy(
            src_ref=source,
            dst_ref=full_grad.at[slot],
            send_sem=gather_send.at[at],
            recv_sem=gather_recv.at[at],
            device_id={"tensor": peer},
            device_id_type=MESH,
        )

    def stage(slot, source, at):
        columns = pl.ds(pl.multiple_of(slot * width, width), width)
        copy = pltpu.make_async_copy(source, grad_v.at[:, columns], local_sem.at[at])
        copy.start()
        return copy

    first = []
    for step in range(1, pairs):
        copy = push(out_grad, me, lax.rem(row + step, pairs) * 2 + side, step)
        copy.start()
        first.append(copy)
    across = push(out_grad, me, partner, 0)
    across.start()
    own_grad = pltpu.make_async_copy(out_grad, full_grad.at[me], local_sem.at[n])
    own_grad.start()
    staged = [stage(me, out_grad, 0)]
    passed = []
    for step in range(1, pairs):
        first[step - 1].wait_recv()
        slot = lax.rem(row + pairs - step, pairs) * 2 + side
        copy = push(full_grad.at[slot], slot, partner, pairs + step)
        copy.start()
        passed.append(copy)
        staged.append(stage(slot, full_grad.at[slot], step))
    pending = start_exchange(n, hidden, token_hidden, send, recv, own)
    across.wait_recv()
    staged.append(stage(partner, full_grad.at[partner], pairs))
    for step in range(1, pairs):
        passed[step - 1].wait_recv()
        slot = lax.rem(row + pairs - step, pairs) * 2 + 1 - side
        staged.append(stage(slot, full_grad.at[slot], pairs + step))
    for copy in staged:
        copy.wait()
    load_weight.wait()

    @pl.loop(0, weight.shape[0] // 256)
    def _(tile):
        rows = pl.ds(pl.multiple_of(tile * 256, 256), 256)
        rot_v[:, rows] = lax.dot_general(
            grad_v[...], weight_v[rows, :], (((1,), (1,)), ((), ())),
            preferred_element_type=jnp.float32,
        ).astype(rot_v.dtype)

    store = pltpu.make_async_copy(rot_v, rot_grad, weight_sem)
    store.start()
    store.wait()
    own_grad.wait()
    for copy in first + passed + [across]:
        copy.wait_send()
    for copy in pending:
        copy.wait()


def round_levels(value):
    largest = jnp.max(jnp.abs(value), axis=-1, keepdims=True)
    spacing = largest * (0.9 / 7.0) + 1e-06
    scaled = value * (1.0 / spacing)
    rest = scaled - jnp.round(scaled)
    square = rest * rest
    wave = jnp.full_like(square, SINE[-1])
    for factor in SINE[-2::-1]:
        wave = wave * square + factor
    return jnp.minimum(scaled - wave * rest, 7.0) * spacing


def rotate_kernel(
    n, quantized, rows_in, table, outgoing, rows_out, incoming,
    in_v, table_v, mid_v, out_v, send, recv, own, local_sem,
):
    load = pltpu.make_async_copy(rows_in, in_v, local_sem.at[0])
    load.start()
    load_table = pltpu.make_async_copy(table, table_v, local_sem.at[1])
    load_table.start()
    greet(n)
    pending = start_exchange(n, outgoing, incoming, send, recv, own)
    load.wait()
    load_table.wait()
    tokens = rows_in.shape[1]
    per = rows_in.shape[2] // PIECE
    scale = 1.0 / math.sqrt(n * per * PIECE)

    @pl.loop(0, n)
    def _(at):
        block = in_v[at]
        stacked = jnp.concatenate(
            [block[:, PIECE * k : PIECE * (k + 1)] for k in range(per)], axis=0
        )
        first = jnp.dot(stacked, table_v[...], preferred_element_type=jnp.float32)
        mid_v[pl.ds(at * per, per)] = first.reshape(per, tokens, PIECE)

    signs = conference()
    order = signs.shape[0]
    lane_tiles = PIECE // GROUP

    @pl.loop(0, tokens // 16 * lane_tiles)
    def _(step):
        rows = pl.ds(pl.multiple_of((step // lane_tiles) * 16, 16), 16)
        lane = (step % lane_tiles) * GROUP
        lanes = pl.ds(pl.multiple_of(lane, GROUP), GROUP)

        def total(i, j, half):
            even, odd = mid_v[i * 4 + j * 2, rows, lanes], mid_v[i * 4 + j * 2 + 1, rows, lanes]
            return even - odd if half else even + odd

        for half in range(2):
            mixed = [[None] * order, [None] * order]
            for i in range(order):
                one, two = total(i, 0, half), total(i, 1, half)
                mixed[0][i] = one + two
                mixed[1][i] = one - two
            for j in range(2):
                for i in range(order):
                    value = mixed[1][i] if j == 0 else -mixed[0][i]
                    for other in range(order):
                        if signs[other, i] > 0:
                            value = value + mixed[j][other]
                        elif signs[other, i] < 0:
                            value = value - mixed[j][other]
                    value = value * scale
                    if quantized:
                        value = round_levels(value)
                    unit = i * 4 + j * 2 + half
                    place = pl.ds(pl.multiple_of(lane + unit % per * PIECE, GROUP), GROUP)
                    out_v[unit // per, rows, place] = value.astype(out_v.dtype)

    store = pltpu.make_async_copy(out_v, rows_out, local_sem.at[0])
    store.start()
    store.wait()
    for copy in pending:
        copy.wait()


def gradient_kernel(
    n, quantized, full_grad, outgoing, grad_down, incoming,
    quant_v, grad_v, down_v, send, recv, own, side_send, side_recv, local_sem,
):
    core = lax.axis_index("dp")
    other = 1 - core
    half = n // 2
    tokens = full_grad.shape[1]
    width = full_grad.shape[2]

    def columns(which):
        return full_grad.at[pl.ds(which * half, half)]

    loads = [
        pltpu.make_async_copy(quantized, quant_v.at[pl.ds(0, n)], local_sem.at[0]),
        pltpu.make_async_copy(columns(core), grad_v.at[0], local_sem.at[1]),
    ]
    for copy in loads:
        copy.start()
    greet(n, sibling=True)
    shared = []
    for at, (source, target) in enumerate(
        [(quantized, quant_v.at[pl.ds(n, n)]), (columns(other), grad_v.at[1])]
    ):
        copy = pltpu.make_async_remote_copy(
            src_ref=source,
            dst_ref=target,
            send_sem=side_send.at[at],
            recv_sem=side_recv.at[at],
            device_id={"dp": other},
            device_id_type=MESH,
        )
        copy.start()
        shared.append(copy)
    pending = start_exchange(n, outgoing, incoming, send, recv, own)
    for copy in loads + shared:
        copy.wait()

    @pl.loop(0, grad_down.shape[0] // 256)
    def _(tile):
        units = pl.ds(pl.multiple_of(tile * 256, 256), 256)
        levels = quant_v[:, :, units].reshape(2, tokens, 256)
        mine, theirs = levels[0].T, levels[1].T
        for at in range(half):
            total = jnp.dot(mine, grad_v[0, at], preferred_element_type=jnp.float32)
            total += jnp.dot(theirs, grad_v[1, at], preferred_element_type=jnp.float32)
            down_v[units, at * width : (at + 1) * width] = total.astype(down_v.dtype)

    store = pltpu.make_async_copy(down_v, grad_down, local_sem.at[0])
    store.start()
    store.wait()
    for copy in pending:
        copy.wait()


def call(kernel, outs, scratch, number, flops, operands):
    dma = pltpu.SemaphoreType.DMA
    return pl.pallas_call(
        kernel,
        out_shape=[jax.ShapeDtypeStruct(shape, jnp.bfloat16) for shape in outs],
        in_specs=[ANY] * len(operands),
        out_specs=[ANY] * len(outs),
        scratch_shapes=[dma(s) if isinstance(s, tuple) else s for s in scratch],
        compiler_params=pltpu.CompilerParams(
            collective_id=number, has_side_effects=True, vmem_limit_bytes=VMEM_LIMIT
        ),
        cost_estimate=pl.CostEstimate(flops=flops, bytes_accessed=40_000_000, transcendentals=0),
    )(*operands)


def with_kernels(n, gate_pre, up_pre, down_weight, out_grad):
    tokens, units = gate_pre.shape
    width, part = out_grad.shape[1], tokens // n
    features = n * width
    per = units // PIECE
    gate_wide = gate_pre.astype(jnp.float32)
    up_wide = up_pre.astype(jnp.float32)
    sigmoid_gate = jax.nn.sigmoid(gate_wide)
    activated = gate_wide * sigmoid_gate
    hidden = (activated * up_wide).astype(jnp.bfloat16).reshape(n, part, units)
    table = sylvester(PIECE).astype(jnp.bfloat16)
    blocks = (n, part, units)
    wide, one = jnp.bfloat16, ()
    exchange = [(n,), (n,), one]

    full_grad, token_hidden, rot_grad = call(
        functools.partial(forward_kernel, n),
        [(n, tokens, width), blocks, (tokens, units)],
        [
            pltpu.VMEM((units, features), wide),
            pltpu.VMEM((tokens, features), wide),
            pltpu.VMEM((tokens, units), wide),
            *exchange, (n,), (n,), (n + 1,), one,
        ],
        1, 2 * tokens * units * features, [hidden, out_grad, down_weight],
    )

    def rotated(rows_in, outgoing, quantized, number):
        return call(
            functools.partial(rotate_kernel, n, quantized),
            [blocks, blocks],
            [
                pltpu.VMEM(blocks, wide),
                pltpu.VMEM((PIECE, PIECE), wide),
                pltpu.VMEM((n * per, part, PIECE), jnp.float32),
                pltpu.VMEM(blocks, wide),
                *exchange, (2,),
            ],
            number, 2 * part * n * units * PIECE, [rows_in, table, outgoing],
        )

    quant_rows, token_grad = rotated(token_hidden, rot_grad.reshape(blocks), True, 2)
    back_rows, quantized = rotated(token_grad, quant_rows, False, 3)
    grad_down, hidden_grad = call(
        functools.partial(gradient_kernel, n),
        [(units, features // 2), blocks],
        [
            pltpu.VMEM((2 * n, part, units), wide),
            pltpu.VMEM((2, n // 2, tokens, width), wide),
            pltpu.VMEM((units, features // 2), wide),
            *exchange, (2,), (2,), (2,),
        ],
        4, 2 * tokens * units * features, [quantized, full_grad, back_rows],
    )
    hid_wide = hidden_grad.reshape(tokens, units).astype(jnp.float32)
    grad_up = (hid_wide * activated).astype(jnp.bfloat16)
    grad_gate = (
        hid_wide * up_wide * sigmoid_gate * (1.0 + gate_wide * (1.0 - sigmoid_gate))
    ).astype(jnp.bfloat16)
    return (grad_gate, grad_up, grad_down)


def choose(n, cores, gate_pre, up_pre, down_weight, out_grad):
    tokens, units = gate_pre.shape
    fits = (
        n % 2 == 0 and n <= 16 and cores == 2
        and tokens % (16 * n) == 0 and units % PIECE == 0 and units % 256 == 0
        and n * units == 28 * HAD_LARGE and out_grad.shape[1] % 128 == 0
    )
    if fits:
        return with_kernels(n, gate_pre, up_pre, down_weight, out_grad)
    return per_device(gate_pre, up_pre, down_weight, out_grad)


def solution(mesh):
    return jax.shard_map(
        functools.partial(choose, mesh.shape["tensor"], mesh.shape["dp"]),
        mesh=mesh,
        in_specs=(
            P(("groups", "dp"), "tensor"),
            P(("groups", "dp"), "tensor"),
            P("tensor", None),
            P(("groups", "dp"), "tensor"),
        ),
        out_specs=(
            P(("groups", "dp"), "tensor"),
            P(("groups", "dp"), "tensor"),
            P(("groups", "tensor"), "dp"),
        ),
        check_vma=False,
    )
```

```python
import functools
import math

import jax
import jax.numpy as jnp
import numpy as np
from jax import lax
from jax.experimental import pallas as pl
from jax.experimental.pallas import tpu as pltpu
from jax.sharding import PartitionSpec as P

HAD_LARGE = 1024
GROUP = 128
PIECE = 512
MESH = pl.DeviceIdType.MESH
ANY = pl.BlockSpec(memory_space=pl.ANY)
VMEM_LIMIT = 60 * 1024 * 1024


def paley_table():
    residues = set((number * number % 13 for number in range(1, 13)))
    core_matrix = np.zeros((14, 14))
    core_matrix[0, 1:] = 1.0
    core_matrix[1:, 0] = 1.0
    for row_index in range(13):
        for col_index in range(13):
            offset = (col_index - row_index) % 13
            if offset != 0:
                core_matrix[row_index + 1, col_index + 1] = 1.0 if offset in residues else -1.0
    upper_block = np.array([[1.0, 1.0], [1.0, -1.0]])
    diagonal_block = np.array([[1.0, -1.0], [-1.0, -1.0]])
    return np.kron(core_matrix, upper_block) + np.kron(np.eye(14), diagonal_block)


def sylvester(matrix_order):
    positions = jnp.arange(matrix_order, dtype=jnp.int32)
    common_bits = jnp.bitwise_and(positions[:, None], positions[None, :])
    parity = jnp.zeros((matrix_order, matrix_order), jnp.int32)
    for bit_shift in range(matrix_order.bit_length() - 1):
        parity = parity + jnp.bitwise_and(jnp.right_shift(common_bits, bit_shift), 1)
    return (1 - 2 * (parity % 2)).astype(jnp.float32)


def rotate(rows_in, small_table, large_table):
    row_count, width = rows_in.shape
    large_order = large_table.shape[0]
    small_order = small_table.shape[0]
    first_section = jnp.dot(
        rows_in.reshape(row_count * small_order, large_order),
        large_table,
        preferred_element_type=jnp.float32,
    )
    first_section = first_section.reshape(row_count, small_order, large_order)
    rotated = jnp.einsum("ac,tad->tcd", small_table, first_section, precision=lax.Precision.HIGHEST)
    return rotated.reshape(row_count, width) * (1.0 / math.sqrt(width))


def quantize(rotated):
    grouped = rotated.reshape(rotated.shape[0], -1, GROUP)
    largest = jnp.max(jnp.abs(grouped), axis=-1, keepdims=True)
    spacing = largest * (0.9 / 7.0) + 1e-06
    scaled = grouped / spacing
    staircase = jnp.minimum(scaled - jnp.sin(2.0 * math.pi * scaled) / (2.0 * math.pi), 7.0)
    return (staircase * spacing).reshape(rotated.shape).astype(jnp.bfloat16)


def per_device(gate_pre, up_pre, down_weight, out_grad):
    small_table = jnp.asarray(paley_table(), jnp.float32)
    large_table = sylvester(HAD_LARGE).astype(jnp.bfloat16)
    gate_wide = gate_pre.astype(jnp.float32)
    up_wide = up_pre.astype(jnp.float32)
    sigmoid_gate = jax.nn.sigmoid(gate_wide)
    activated = gate_wide * sigmoid_gate
    hidden = (activated * up_wide).astype(jnp.bfloat16)
    full_grad = lax.all_gather(out_grad, "tensor", axis=1, tiled=True)
    rot_grad = lax.dot_general(
        full_grad, down_weight, (((1,), (1,)), ((), ())), preferred_element_type=jnp.float32
    ).astype(jnp.bfloat16)
    token_hidden = lax.all_to_all(hidden, "tensor", split_axis=0, concat_axis=1, tiled=True)
    quant_rows = quantize(rotate(token_hidden, small_table, large_table))
    quantized = lax.all_to_all(quant_rows, "tensor", split_axis=1, concat_axis=0, tiled=True)
    token_grad = lax.all_to_all(rot_grad, "tensor", split_axis=0, concat_axis=1, tiled=True)
    back_rows = rotate(token_grad, small_table.T, large_table.T).astype(jnp.bfloat16)
    hidden_grad = lax.all_to_all(back_rows, "tensor", split_axis=1, concat_axis=0, tiled=True)
    partial_grad = lax.dot_general(
        quantized, full_grad, (((0,), (0,)), ((), ())), preferred_element_type=jnp.float32
    )
    grad_down = lax.psum_scatter(partial_grad, "dp", scatter_dimension=1, tiled=True).astype(
        jnp.bfloat16
    )
    hid_wide = hidden_grad.astype(jnp.float32)
    grad_up = (hid_wide * activated).astype(jnp.bfloat16)
    grad_gate = (
        hid_wide * up_wide * sigmoid_gate * (1.0 + gate_wide * (1.0 - sigmoid_gate))
    ).astype(jnp.bfloat16)
    return (grad_gate, grad_up, grad_down)


def conference():
    signs = paley_table()[::2, ::2].copy()
    np.fill_diagonal(signs, 0.0)
    return signs


SINE = tuple((0.9999999944722885, -6.579735439437039, 12.987842893122675, -12.207428862951517, 6.6870661467168215, -2.3663670610371574, 0.5091905912043592))


def greet(n, sibling=False):
    me = lax.axis_index("tensor")
    barrier = pltpu.get_barrier_semaphore()
    for step in range(1, n):
        pl.semaphore_signal(
            barrier, inc=1, device_id={"tensor": lax.rem(me + step, n)}, device_id_type=MESH
        )
    if sibling:
        other = 1 - lax.axis_index("dp")
        pl.semaphore_signal(barrier, inc=1, device_id={"dp": other}, device_id_type=MESH)
    pl.semaphore_wait(barrier, n if sibling else n - 1)


def round_levels(value):
    largest = jnp.max(jnp.abs(value), axis=-1, keepdims=True)
    spacing = largest * (0.9 / 7.0) + 1e-06
    scaled = value * (1.0 / spacing)
    rest = scaled - jnp.round(scaled)
    square = rest * rest
    wave = jnp.full_like(square, SINE[-1])
    for factor in SINE[-2::-1]:
        wave = wave * square + factor
    return jnp.minimum(scaled - wave * rest, 7.0) * spacing


def exchange(n, source, target, send, recv):
    me = lax.axis_index("tensor")
    copies = []
    for step in sorted(range(1, n), key=lambda s: abs(s - n // 2)):
        peer = lax.rem(me + step, n)
        copy = pltpu.make_async_remote_copy(
            src_ref=source.at[peer],
            dst_ref=target.at[me],
            send_sem=send.at[step],
            recv_sem=recv.at[step],
            device_id={"tensor": peer},
            device_id_type=MESH,
        )
        copy.start()
        copies.append(copy)
    local = pltpu.make_async_copy(source.at[me], target.at[me], recv.at[0])
    local.start()
    return copies, local


def arrived(pending):
    for copy in pending[0]:
        copy.wait_recv()
    pending[1].wait()


def gather_columns(n, out_grad, grad_v, sems, between):
    me = lax.axis_index("tensor")
    line = n // 2
    width = out_grad.shape[1]
    row, side = me // 2, lax.rem(me, 2)

    def slot(at_row, at_side):
        place = lax.rem(at_row + line, line) * 2 + at_side
        return grad_v.at[:, pl.ds(pl.multiple_of(place * width, width), width)]

    def push(source_row, peer, at):
        return pltpu.make_async_remote_copy(
            src_ref=slot(source_row, side),
            dst_ref=slot(source_row, side),
            send_sem=sems.at[0, at],
            recv_sem=sems.at[1, at],
            device_id={"tensor": peer},
            device_id_type=MESH,
        )

    def along(sign, hop):
        peer = lax.rem(row + sign + line, line) * 2 + side
        return push(row - sign * (hop - 1), peer, hop if sign > 0 else line + hop)

    def across(sign, hop):
        at = 2 * line + (0 if hop == 0 else hop if sign > 0 else line + hop)
        return push(row - sign * hop, row * 2 + 1 - side, at)

    def has(sign, hop):
        return row - hop >= 0 if sign > 0 else row + hop < line

    for sign in (1, -1):
        pl.when(has(-sign, 1))(lambda sign=sign: along(sign, 1).start())
    across(1, 0).start()
    for hop in range(1, line):
        for sign in (1, -1):

            @pl.when(has(sign, hop))
            def _(sign=sign, hop=hop):
                along(sign, hop).wait_recv()
                if hop + 1 < line:
                    pl.when(has(-sign, 1))(lambda: along(sign, hop + 1).start())
                across(sign, hop).start()

        if hop == 1:
            pending = between()
    across(1, 0).wait()
    for hop in range(1, line):
        for sign in (1, -1):

            @pl.when(has(sign, hop))
            def _(sign=sign, hop=hop):
                across(sign, hop).wait()

            @pl.when(has(sign, hop - 1) & has(-sign, 1))
            def _(sign=sign, hop=hop):
                along(sign, hop).wait_send()

    return pending


def rotate_pieces(n, quantized, in_v, table_v, mid_v, out_v):
    tokens = in_v.shape[1]
    per = in_v.shape[2] // PIECE
    scale = 1.0 / math.sqrt(n * per * PIECE)

    @pl.loop(0, n)
    def _(at):
        block = in_v[at]
        stacked = jnp.concatenate(
            [block[:, PIECE * k : PIECE * (k + 1)] for k in range(per)], axis=0
        )
        first = jnp.dot(stacked, table_v[...], preferred_element_type=jnp.float32)
        mid_v[pl.ds(at * per, per)] = first.reshape(per, tokens, PIECE)

    signs = conference()
    order = signs.shape[0]
    lane_tiles = PIECE // GROUP

    @pl.loop(0, tokens // 16 * lane_tiles)
    def _(step):
        rows = pl.ds(pl.multiple_of((step // lane_tiles) * 16, 16), 16)
        lane = (step % lane_tiles) * GROUP
        lanes = pl.ds(pl.multiple_of(lane, GROUP), GROUP)

        def total(i, j, half):
            even, odd = mid_v[i * 4 + j * 2, rows, lanes], mid_v[i * 4 + j * 2 + 1, rows, lanes]
            return even - odd if half else even + odd

        for half in range(2):
            mixed = [[None] * order, [None] * order]
            for i in range(order):
                one, two = total(i, 0, half), total(i, 1, half)
                mixed[0][i] = one + two
                mixed[1][i] = one - two
            for j in range(2):
                for i in range(order):
                    value = mixed[1][i] if j == 0 else -mixed[0][i]
                    for other in range(order):
                        if signs[other, i] > 0:
                            value = value + mixed[j][other]
                        elif signs[other, i] < 0:
                            value = value - mixed[j][other]
                    value = value * scale
                    if quantized:
                        value = round_levels(value)
                    unit = i * 4 + j * 2 + half
                    place = pl.ds(pl.multiple_of(lane + unit % per * PIECE, GROUP), GROUP)
                    out_v[unit // per, rows, place] = value.astype(out_v.dtype)


def whole_kernel(
    n, gate, up, out_grad, weight, table, hidden_grad, grad_down,
    hidden_v, token_v, rot_v, back_in_v, mid_v, out_v, back_v, quant_v,
    grad_v, side_grad_v, weight_v, down_v, table_v,
    gather_sem, send, recv, side_send, side_recv, local_sem, weight_sem, down_sem,
):
    me = lax.axis_index("tensor")
    core = lax.axis_index("dp")
    tokens, width = out_grad.shape
    part = tokens // n
    features = n * width
    half = features // 2
    tiles = weight.shape[0] // 256
    mine = pl.ds(pl.multiple_of(me * width, width), width)
    loads = [
        pltpu.make_async_copy(source, target, local_sem.at[at])
        for at, (source, target) in enumerate(
            [(gate, out_v), (up, back_v), (table, table_v), (out_grad, grad_v.at[:, mine])]
        )
    ]
    for copy in loads:
        copy.start()

    def fetch(tile):
        slot = lax.rem(tile, 2)
        rows = pl.ds(pl.multiple_of(tile * 256, 256), 256)
        return pltpu.make_async_copy(weight.at[rows], weight_v.at[slot], weight_sem.at[slot])

    fetch(0).start()
    greet(n, sibling=True)
    loads[3].wait()

    def make_hidden():
        loads[0].wait()
        loads[1].wait()

        @pl.loop(0, n * part // 16)
        def _(step):
            at = step // (part // 16)
            rows = pl.ds(pl.multiple_of(step % (part // 16) * 16, 16), 16)
            wide = out_v[at, rows, :].astype(jnp.float32)
            active = wide * jax.nn.sigmoid(wide)
            hidden_v[at, rows, :] = (active * back_v[at, rows, :].astype(jnp.float32)).astype(
                hidden_v.dtype
            )

        return exchange(n, hidden_v, token_v, send.at[0], recv.at[0])

    to_tokens = gather_columns(n, out_grad, grad_v, gather_sem, make_hidden)

    @pl.loop(0, tiles)
    def _(tile):
        pl.when(tile + 1 < tiles)(lambda: fetch(tile + 1).start())
        fetch(tile).wait()
        units = pl.ds(pl.multiple_of(tile * 256, 256), 256)
        product = lax.dot_general(
            grad_v[...], weight_v[lax.rem(tile, 2)], (((1,), (1,)), ((), ())),
            preferred_element_type=jnp.float32,
        )
        rot_v[:, :, units] = product.astype(rot_v.dtype).reshape(n, part, 256)

    grads_to_tokens = exchange(n, rot_v, back_in_v, send.at[1], recv.at[1])

    def beside(which):
        return grad_v.at[:, pl.ds(pl.multiple_of(which * half, half), half)]

    def to_sibling(source, target, at):
        copy = pltpu.make_async_remote_copy(
            src_ref=source,
            dst_ref=target,
            send_sem=side_send.at[at],
            recv_sem=side_recv.at[at],
            device_id={"dp": 1 - core},
            device_id_type=MESH,
        )
        copy.start()
        return copy

    side_grad = to_sibling(beside(1 - core), side_grad_v, 0)
    loads[2].wait()
    arrived(to_tokens)
    rotate_pieces(n, True, token_v, table_v, mid_v, out_v)
    own_levels = quant_v.at[pl.ds(0, n)]
    levels = exchange(n, out_v, own_levels, send.at[2], recv.at[2])
    arrived(grads_to_tokens)
    rotate_pieces(n, False, back_in_v, table_v, mid_v, back_v)
    grads_back = exchange(n, back_v, hidden_grad, send.at[3], recv.at[3])
    arrived(levels)
    side_levels = to_sibling(own_levels, quant_v.at[pl.ds(n, n)], 1)
    side_grad.wait()
    side_levels.wait()

    def write(tile):
        slot = lax.rem(tile, 2)
        rows = pl.ds(pl.multiple_of(tile * 256, 256), 256)
        return pltpu.make_async_copy(down_v.at[slot], grad_down.at[rows], down_sem.at[slot])

    own_columns = pl.ds(pl.multiple_of(core * half, half), half)

    @pl.loop(0, tiles)
    def _(tile):
        pl.when(tile >= 2)(lambda: write(tile - 2).wait())
        units = pl.ds(pl.multiple_of(tile * 256, 256), 256)
        rows = quant_v[:, :, units].reshape(2, tokens, 256)
        total = jnp.dot(rows[0].T, grad_v[:, own_columns], preferred_element_type=jnp.float32)
        total += jnp.dot(rows[1].T, side_grad_v[...], preferred_element_type=jnp.float32)
        down_v[lax.rem(tile, 2)] = total.astype(down_v.dtype)
        write(tile).start()

    for tile in range(max(tiles - 2, 0), tiles):
        write(tile).wait()
    arrived(grads_back)
    for copies, _ in (to_tokens, grads_to_tokens, levels, grads_back):
        for copy in copies:
            copy.wait_send()


def with_kernel(n, gate_pre, up_pre, down_weight, out_grad):
    tokens, units = gate_pre.shape
    width, part = out_grad.shape[1], tokens // n
    features = n * width
    blocks = (n, part, units)
    wide = jnp.bfloat16
    table = jnp.asarray(functools.reduce(np.kron, [[[1.0, 1.0], [1.0, -1.0]]] * (PIECE.bit_length() - 1)), wide)
    dma = pltpu.SemaphoreType.DMA
    keep = pltpu.VMEM(blocks, wide)
    hidden_grad, grad_down = pl.pallas_call(
        functools.partial(whole_kernel, n),
        out_shape=[
            jax.ShapeDtypeStruct(blocks, wide),
            jax.ShapeDtypeStruct((units, features // 2), wide),
        ],
        in_specs=[ANY] * 5,
        out_specs=[ANY] * 2,
        scratch_shapes=[
            keep, keep, keep, keep,
            pltpu.VMEM((n * units // PIECE, part, PIECE), jnp.float32),
            keep, keep,
            pltpu.VMEM((2 * n, part, units), wide),
            pltpu.VMEM((tokens, features), wide),
            pltpu.VMEM((tokens, features // 2), wide),
            pltpu.VMEM((2, 256, features), wide),
            pltpu.VMEM((2, 256, features // 2), wide),
            pltpu.VMEM((PIECE, PIECE), wide),
            dma((2, 2 * n)), dma((4, n)), dma((4, n)), dma((2,)), dma((2,)),
            dma((4,)), dma((2,)), dma((2,)),
        ],
        compiler_params=pltpu.CompilerParams(
            collective_id=1, has_side_effects=True, vmem_limit_bytes=VMEM_LIMIT
        ),
        cost_estimate=pl.CostEstimate(
            flops=4 * tokens * units * features, bytes_accessed=60_000_000, transcendentals=0
        ),
    )(gate_pre.reshape(blocks), up_pre.reshape(blocks), out_grad, down_weight, table)
    gate_wide = gate_pre.astype(jnp.float32)
    up_wide = up_pre.astype(jnp.float32)
    sigmoid_gate = jax.nn.sigmoid(gate_wide)
    activated = gate_wide * sigmoid_gate
    hid_wide = hidden_grad.reshape(tokens, units).astype(jnp.float32)
    grad_up = (hid_wide * activated).astype(wide)
    grad_gate = (
        hid_wide * up_wide * sigmoid_gate * (1.0 + gate_wide * (1.0 - sigmoid_gate))
    ).astype(wide)
    return (grad_gate, grad_up, grad_down)


def choose(n, cores, gate_pre, up_pre, down_weight, out_grad):
    tokens, units = gate_pre.shape
    fits = (
        n % 2 == 0 and n <= 16 and cores == 2
        and tokens % (16 * n) == 0 and units % PIECE == 0 and units % 256 == 0
        and n * units == 28 * HAD_LARGE and out_grad.shape[1] % 128 == 0
    )
    if fits:
        return with_kernel(n, gate_pre, up_pre, down_weight, out_grad)
    return per_device(gate_pre, up_pre, down_weight, out_grad)


def solution(mesh):
    return jax.shard_map(
        functools.partial(choose, mesh.shape["tensor"], mesh.shape["dp"]),
        mesh=mesh,
        in_specs=(
            P(("groups", "dp"), "tensor"),
            P(("groups", "dp"), "tensor"),
            P("tensor", None),
            P(("groups", "dp"), "tensor"),
        ),
        out_specs=(
            P(("groups", "dp"), "tensor"),
            P(("groups", "dp"), "tensor"),
            P(("groups", "tensor"), "dp"),
        ),
        check_vma=False,
    )
```

```python
import functools
import math

import jax
import jax.numpy as jnp
import numpy as np
from jax import lax
from jax.experimental import pallas as pl
from jax.experimental.pallas import tpu as pltpu
from jax.sharding import PartitionSpec as P

HAD_LARGE = 1024
GROUP = 128
PIECE = 512
CHUNK = 16
MESH = pl.DeviceIdType.MESH
ANY = pl.BlockSpec(memory_space=pl.ANY)
VMEM_LIMIT = 60 * 1024 * 1024


def paley_table():
    residues = set((number * number % 13 for number in range(1, 13)))
    core_matrix = np.zeros((14, 14))
    core_matrix[0, 1:] = 1.0
    core_matrix[1:, 0] = 1.0
    for row_index in range(13):
        for col_index in range(13):
            offset = (col_index - row_index) % 13
            if offset != 0:
                core_matrix[row_index + 1, col_index + 1] = 1.0 if offset in residues else -1.0
    upper_block = np.array([[1.0, 1.0], [1.0, -1.0]])
    diagonal_block = np.array([[1.0, -1.0], [-1.0, -1.0]])
    return np.kron(core_matrix, upper_block) + np.kron(np.eye(14), diagonal_block)


def sylvester(matrix_order):
    positions = jnp.arange(matrix_order, dtype=jnp.int32)
    common_bits = jnp.bitwise_and(positions[:, None], positions[None, :])
    parity = jnp.zeros((matrix_order, matrix_order), jnp.int32)
    for bit_shift in range(matrix_order.bit_length() - 1):
        parity = parity + jnp.bitwise_and(jnp.right_shift(common_bits, bit_shift), 1)
    return (1 - 2 * (parity % 2)).astype(jnp.float32)


def rotate(rows_in, small_table, large_table):
    row_count, width = rows_in.shape
    large_order = large_table.shape[0]
    small_order = small_table.shape[0]
    first_section = jnp.dot(
        rows_in.reshape(row_count * small_order, large_order),
        large_table,
        preferred_element_type=jnp.float32,
    )
    first_section = first_section.reshape(row_count, small_order, large_order)
    rotated = jnp.einsum("ac,tad->tcd", small_table, first_section, precision=lax.Precision.HIGHEST)
    return rotated.reshape(row_count, width) * (1.0 / math.sqrt(width))


def quantize(rotated):
    grouped = rotated.reshape(rotated.shape[0], -1, GROUP)
    largest = jnp.max(jnp.abs(grouped), axis=-1, keepdims=True)
    spacing = largest * (0.9 / 7.0) + 1e-06
    scaled = grouped / spacing
    staircase = jnp.minimum(scaled - jnp.sin(2.0 * math.pi * scaled) / (2.0 * math.pi), 7.0)
    return (staircase * spacing).reshape(rotated.shape).astype(jnp.bfloat16)


def per_device(gate_pre, up_pre, down_weight, out_grad):
    small_table = jnp.asarray(paley_table(), jnp.float32)
    large_table = sylvester(HAD_LARGE).astype(jnp.bfloat16)
    gate_wide = gate_pre.astype(jnp.float32)
    up_wide = up_pre.astype(jnp.float32)
    sigmoid_gate = jax.nn.sigmoid(gate_wide)
    activated = gate_wide * sigmoid_gate
    hidden = (activated * up_wide).astype(jnp.bfloat16)
    full_grad = lax.all_gather(out_grad, "tensor", axis=1, tiled=True)
    rot_grad = lax.dot_general(
        full_grad, down_weight, (((1,), (1,)), ((), ())), preferred_element_type=jnp.float32
    ).astype(jnp.bfloat16)
    token_hidden = lax.all_to_all(hidden, "tensor", split_axis=0, concat_axis=1, tiled=True)
    quant_rows = quantize(rotate(token_hidden, small_table, large_table))
    quantized = lax.all_to_all(quant_rows, "tensor", split_axis=1, concat_axis=0, tiled=True)
    token_grad = lax.all_to_all(rot_grad, "tensor", split_axis=0, concat_axis=1, tiled=True)
    back_rows = rotate(token_grad, small_table.T, large_table.T).astype(jnp.bfloat16)
    hidden_grad = lax.all_to_all(back_rows, "tensor", split_axis=1, concat_axis=0, tiled=True)
    partial_grad = lax.dot_general(
        quantized, full_grad, (((0,), (0,)), ((), ())), preferred_element_type=jnp.float32
    )
    grad_down = lax.psum_scatter(partial_grad, "dp", scatter_dimension=1, tiled=True).astype(
        jnp.bfloat16
    )
    hid_wide = hidden_grad.astype(jnp.float32)
    grad_up = (hid_wide * activated).astype(jnp.bfloat16)
    grad_gate = (
        hid_wide * up_wide * sigmoid_gate * (1.0 + gate_wide * (1.0 - sigmoid_gate))
    ).astype(jnp.bfloat16)
    return (grad_gate, grad_up, grad_down)


def conference():
    signs = paley_table()[::2, ::2].copy()
    np.fill_diagonal(signs, 0.0)
    return signs


SINE = tuple((0.9999999944722885, -6.579735439437039, 12.987842893122675, -12.207428862951517, 6.6870661467168215, -2.3663670610371574, 0.5091905912043592))


def greet(n, sibling=False):
    me = lax.axis_index("tensor")
    barrier = pltpu.get_barrier_semaphore()
    for step in range(1, n):
        pl.semaphore_signal(
            barrier, inc=1, device_id={"tensor": lax.rem(me + step, n)}, device_id_type=MESH
        )
    if sibling:
        other = 1 - lax.axis_index("dp")
        pl.semaphore_signal(barrier, inc=1, device_id={"dp": other}, device_id_type=MESH)
    pl.semaphore_wait(barrier, n if sibling else n - 1)


def round_levels(value):
    largest = jnp.max(jnp.abs(value), axis=-1, keepdims=True)
    spacing = largest * (0.9 / 7.0) + 1e-06
    scaled = value * (1.0 / spacing)
    rest = scaled - jnp.round(scaled)
    square = rest * rest
    wave = jnp.full_like(square, SINE[-1])
    for factor in SINE[-2::-1]:
        wave = wave * square + factor
    return jnp.minimum(scaled - wave * rest, 7.0) * spacing


def exchange_copies(n, chunk, source, target, send, recv):
    me = lax.axis_index("tensor")
    rows = pl.ds(pl.multiple_of(chunk * CHUNK, CHUNK), CHUNK)
    copies = []
    for step in sorted(range(1, n), key=lambda s: abs(s - n // 2)):
        peer = lax.rem(me + step, n)
        copies.append(
            pltpu.make_async_remote_copy(
                src_ref=source.at[peer, rows],
                dst_ref=target.at[me, rows],
                send_sem=send.at[chunk, step],
                recv_sem=recv.at[chunk, step],
                device_id={"tensor": peer},
                device_id_type=MESH,
            )
        )
    local = pltpu.make_async_copy(
        source.at[me, rows], target.at[me, rows], recv.at[chunk, 0]
    )
    return copies, local


def exchange(n, chunk, *refs):
    copies, local = exchange_copies(n, chunk, *refs)
    for copy in copies:
        copy.start()
    local.start()


def arrived(n, chunk, *refs):
    copies, local = exchange_copies(n, chunk, *refs)
    for copy in copies:
        copy.wait_recv()
    local.wait()


def sent(n, chunk, *refs):
    for copy in exchange_copies(n, chunk, *refs)[0]:
        copy.wait_send()


def each_chunk(action, n, *refs):
    @pl.loop(0, refs[0].shape[1] // CHUNK)
    def _(chunk):
        action(n, chunk, *refs)


def gather_columns(n, out_grad, grad_v, sems, meanwhile, between):
    me = lax.axis_index("tensor")
    line = n // 2
    width = out_grad.shape[1]
    row, side = me // 2, lax.rem(me, 2)

    def slot(at_row, at_side):
        place = lax.rem(at_row + line, line) * 2 + at_side
        return grad_v.at[:, pl.ds(pl.multiple_of(place * width, width), width)]

    def push(source_row, peer, at):
        return pltpu.make_async_remote_copy(
            src_ref=slot(source_row, side),
            dst_ref=slot(source_row, side),
            send_sem=sems.at[0, at],
            recv_sem=sems.at[1, at],
            device_id={"tensor": peer},
            device_id_type=MESH,
        )

    def along(sign, hop):
        peer = lax.rem(row + sign + line, line) * 2 + side
        return push(row - sign * (hop - 1), peer, hop if sign > 0 else line + hop)

    def across(sign, hop):
        at = 2 * line + (0 if hop == 0 else hop if sign > 0 else line + hop)
        return push(row - sign * hop, row * 2 + 1 - side, at)

    def has(sign, hop):
        return row - hop >= 0 if sign > 0 else row + hop < line

    for sign in (1, -1):
        pl.when(has(-sign, 1))(lambda sign=sign: along(sign, 1).start())
    across(1, 0).start()
    meanwhile()
    for hop in range(1, line):
        for sign in (1, -1):

            @pl.when(has(sign, hop))
            def _(sign=sign, hop=hop):
                along(sign, hop).wait_recv()
                if hop + 1 < line:
                    pl.when(has(-sign, 1))(lambda: along(sign, hop + 1).start())
                across(sign, hop).start()

        if hop == line // 2:
            between()
    across(1, 0).wait()
    for hop in range(1, line):
        for sign in (1, -1):

            @pl.when(has(sign, hop))
            def _(sign=sign, hop=hop):
                across(sign, hop).wait()

            @pl.when(has(sign, hop - 1) & has(-sign, 1))
            def _(sign=sign, hop=hop):
                along(sign, hop).wait_send()


def rotate_pieces(n, quantized, chunk, in_v, table_v, mid_v, out_v):
    tokens = CHUNK
    per = in_v.shape[2] // PIECE
    scale = 1.0 / math.sqrt(n * per * PIECE)
    rows = pl.ds(pl.multiple_of(chunk * CHUNK, CHUNK), CHUNK)
    stacked = jnp.concatenate(
        [
            in_v[at, rows, PIECE * k : PIECE * (k + 1)]
            for at in range(n)
            for k in range(per)
        ],
        axis=0,
    )
    first = jnp.dot(stacked, table_v[...], preferred_element_type=jnp.float32)
    mid_v[...] = first.reshape(n * per, tokens, PIECE)

    signs = conference()
    order = signs.shape[0]
    lane_tiles = PIECE // GROUP

    @pl.loop(0, lane_tiles)
    def _(step):
        lane = step * GROUP
        lanes = pl.ds(pl.multiple_of(lane, GROUP), GROUP)

        def total(i, j, half):
            even, odd = mid_v[i * 4 + j * 2, :, lanes], mid_v[i * 4 + j * 2 + 1, :, lanes]
            return even - odd if half else even + odd

        for half in range(2):
            mixed = [[None] * order, [None] * order]
            for i in range(order):
                one, two = total(i, 0, half), total(i, 1, half)
                mixed[0][i] = one + two
                mixed[1][i] = one - two
            for j in range(2):
                for i in range(order):
                    value = mixed[1][i] if j == 0 else -mixed[0][i]
                    for other in range(order):
                        if signs[other, i] > 0:
                            value = value + mixed[j][other]
                        elif signs[other, i] < 0:
                            value = value - mixed[j][other]
                    value = value * scale
                    if quantized:
                        value = round_levels(value)
                    unit = i * 4 + j * 2 + half
                    place = pl.ds(pl.multiple_of(lane + unit % per * PIECE, GROUP), GROUP)
                    out_v[unit // per, rows, place] = value.astype(out_v.dtype)


def whole_kernel(
    n, gate, up, out_grad, weight, table, hidden_grad, grad_down,
    hidden_v, token_v, rot_v, back_in_v, mid_v, out_v, back_v, quant_v,
    grad_v, side_grad_v, weight_v, down_v, table_v,
    gather_sem, send, recv, side_send, side_recv, local_sem, weight_sem, down_sem,
):
    me = lax.axis_index("tensor")
    core = lax.axis_index("dp")
    tokens, width = out_grad.shape
    part = tokens // n
    features = n * width
    half = features // 2
    tiles = weight.shape[0] // 256
    mine = pl.ds(pl.multiple_of(me * width, width), width)
    loads = [
        pltpu.make_async_copy(source, target, local_sem.at[at])
        for at, (source, target) in enumerate(
            [(gate, out_v), (up, back_v), (table, table_v), (out_grad, grad_v.at[:, mine])]
        )
    ]
    for copy in loads:
        copy.start()

    def fetch(tile):
        slot = lax.rem(tile, 2)
        rows = pl.ds(pl.multiple_of(tile * 256, 256), 256)
        return pltpu.make_async_copy(weight.at[rows], weight_v.at[slot], weight_sem.at[slot])

    fetch(0).start()
    greet(n, sibling=True)
    loads[3].wait()

    to_tokens, grads_to_tokens, levels, grads_back = [
        (source, target, send.at[at], recv.at[at])
        for at, (source, target) in enumerate(
            [
                (hidden_v, token_v),
                (rot_v, back_in_v),
                (out_v, quant_v.at[pl.ds(0, n)]),
                (back_v, hidden_grad),
            ]
        )
    ]

    def make_hidden():
        loads[0].wait()
        loads[1].wait()

        @pl.loop(0, n * part // 16)
        def _(step):
            at = step // (part // 16)
            rows = pl.ds(pl.multiple_of(step % (part // 16) * 16, 16), 16)
            wide = out_v[at, rows, :].astype(jnp.float32)
            active = wide * jax.nn.sigmoid(wide)
            hidden_v[at, rows, :] = (active * back_v[at, rows, :].astype(jnp.float32)).astype(
                hidden_v.dtype
            )

    def send_hidden():
        each_chunk(exchange, n, *to_tokens)

    gather_columns(n, out_grad, grad_v, gather_sem, make_hidden, send_hidden)

    @pl.loop(0, tiles)
    def _(tile):
        pl.when(tile + 1 < tiles)(lambda: fetch(tile + 1).start())
        fetch(tile).wait()
        units = pl.ds(pl.multiple_of(tile * 256, 256), 256)
        product = lax.dot_general(
            grad_v[...], weight_v[lax.rem(tile, 2)], (((1,), (1,)), ((), ())),
            preferred_element_type=jnp.float32,
        )
        rot_v[:, :, units] = product.astype(rot_v.dtype).reshape(n, part, 256)

    each_chunk(exchange, n, *grads_to_tokens)

    def beside(which):
        return grad_v.at[:, pl.ds(pl.multiple_of(which * half, half), half)]

    def to_sibling(source, target, at):
        copy = pltpu.make_async_remote_copy(
            src_ref=source,
            dst_ref=target,
            send_sem=side_send.at[at],
            recv_sem=side_recv.at[at],
            device_id={"dp": 1 - core},
            device_id_type=MESH,
        )
        copy.start()
        return copy

    side_grad = to_sibling(beside(1 - core), side_grad_v, 0)
    loads[2].wait()

    @pl.loop(0, part // CHUNK)
    def _(chunk):
        arrived(n, chunk, *to_tokens)
        rotate_pieces(n, True, chunk, token_v, table_v, mid_v, out_v)
        exchange(n, chunk, *levels)

    @pl.loop(0, part // CHUNK)
    def _(chunk):
        arrived(n, chunk, *grads_to_tokens)
        rotate_pieces(n, False, chunk, back_in_v, table_v, mid_v, back_v)
        exchange(n, chunk, *grads_back)

    each_chunk(arrived, n, *levels)
    side_levels = to_sibling(quant_v.at[pl.ds(0, n)], quant_v.at[pl.ds(n, n)], 1)
    side_grad.wait()
    side_levels.wait()

    def write(tile):
        slot = lax.rem(tile, 2)
        rows = pl.ds(pl.multiple_of(tile * 256, 256), 256)
        return pltpu.make_async_copy(down_v.at[slot], grad_down.at[rows], down_sem.at[slot])

    own_columns = pl.ds(pl.multiple_of(core * half, half), half)

    @pl.loop(0, tiles)
    def _(tile):
        pl.when(tile >= 2)(lambda: write(tile - 2).wait())
        units = pl.ds(pl.multiple_of(tile * 256, 256), 256)
        rows = quant_v[:, :, units].reshape(2, tokens, 256)
        total = jnp.dot(rows[0].T, grad_v[:, own_columns], preferred_element_type=jnp.float32)
        total += jnp.dot(rows[1].T, side_grad_v[...], preferred_element_type=jnp.float32)
        down_v[lax.rem(tile, 2)] = total.astype(down_v.dtype)
        write(tile).start()

    for tile in range(max(tiles - 2, 0), tiles):
        write(tile).wait()
    each_chunk(arrived, n, *grads_back)
    for refs in (to_tokens, grads_to_tokens, levels, grads_back):
        each_chunk(sent, n, *refs)


def with_kernel(n, gate_pre, up_pre, down_weight, out_grad):
    tokens, units = gate_pre.shape
    width, part = out_grad.shape[1], tokens // n
    features = n * width
    blocks = (n, part, units)
    wide = jnp.bfloat16
    table = jnp.asarray(functools.reduce(np.kron, [[[1.0, 1.0], [1.0, -1.0]]] * (PIECE.bit_length() - 1)), wide)
    dma = pltpu.SemaphoreType.DMA
    keep = pltpu.VMEM(blocks, wide)
    hidden_grad, grad_down = pl.pallas_call(
        functools.partial(whole_kernel, n),
        out_shape=[
            jax.ShapeDtypeStruct(blocks, wide),
            jax.ShapeDtypeStruct((units, features // 2), wide),
        ],
        in_specs=[ANY] * 5,
        out_specs=[ANY] * 2,
        scratch_shapes=[
            keep, keep, keep, keep,
            pltpu.VMEM((n * units // PIECE, CHUNK, PIECE), jnp.float32),
            keep, keep,
            pltpu.VMEM((2 * n, part, units), wide),
            pltpu.VMEM((tokens, features), wide),
            pltpu.VMEM((tokens, features // 2), wide),
            pltpu.VMEM((2, 256, features), wide),
            pltpu.VMEM((2, 256, features // 2), wide),
            pltpu.VMEM((PIECE, PIECE), wide),
            dma((2, 2 * n)), dma((4, part // CHUNK, n)), dma((4, part // CHUNK, n)), dma((2,)), dma((2,)),
            dma((4,)), dma((2,)), dma((2,)),
        ],
        compiler_params=pltpu.CompilerParams(
            collective_id=1, has_side_effects=True, vmem_limit_bytes=VMEM_LIMIT
        ),
        cost_estimate=pl.CostEstimate(
            flops=4 * tokens * units * features, bytes_accessed=60_000_000, transcendentals=0
        ),
    )(gate_pre.reshape(blocks), up_pre.reshape(blocks), out_grad, down_weight, table)
    gate_wide = gate_pre.astype(jnp.float32)
    up_wide = up_pre.astype(jnp.float32)
    sigmoid_gate = jax.nn.sigmoid(gate_wide)
    activated = gate_wide * sigmoid_gate
    hid_wide = hidden_grad.reshape(tokens, units).astype(jnp.float32)
    grad_up = (hid_wide * activated).astype(wide)
    grad_gate = (
        hid_wide * up_wide * sigmoid_gate * (1.0 + gate_wide * (1.0 - sigmoid_gate))
    ).astype(wide)
    return (grad_gate, grad_up, grad_down)


def choose(n, cores, gate_pre, up_pre, down_weight, out_grad):
    tokens, units = gate_pre.shape
    fits = (
        n % 2 == 0 and 4 <= n <= 16 and cores == 2
        and tokens % (CHUNK * n) == 0 and units % PIECE == 0 and units % 256 == 0
        and n * units == 28 * HAD_LARGE and out_grad.shape[1] % 128 == 0
    )
    if fits:
        return with_kernel(n, gate_pre, up_pre, down_weight, out_grad)
    return per_device(gate_pre, up_pre, down_weight, out_grad)


def solution(mesh):
    return jax.shard_map(
        functools.partial(choose, mesh.shape["tensor"], mesh.shape["dp"]),
        mesh=mesh,
        in_specs=(
            P(("groups", "dp"), "tensor"),
            P(("groups", "dp"), "tensor"),
            P("tensor", None),
            P(("groups", "dp"), "tensor"),
        ),
        out_specs=(
            P(("groups", "dp"), "tensor"),
            P(("groups", "dp"), "tensor"),
            P(("groups", "tensor"), "dp"),
        ),
        check_vma=False,
    )
```

```python
import functools
import math

import jax
import jax.numpy as jnp
import numpy as np
from jax import lax
from jax.experimental import pallas as pl
from jax.experimental.pallas import tpu as pltpu
from jax.sharding import PartitionSpec as P

HAD_LARGE = 1024
GROUP = 128
PIECE = 512
CHUNK = 16
MESH = pl.DeviceIdType.MESH
ANY = pl.BlockSpec(memory_space=pl.ANY)
VMEM_LIMIT = 60 * 1024 * 1024


def paley_table():
    residues = set((number * number % 13 for number in range(1, 13)))
    core_matrix = np.zeros((14, 14))
    core_matrix[0, 1:] = 1.0
    core_matrix[1:, 0] = 1.0
    for row_index in range(13):
        for col_index in range(13):
            offset = (col_index - row_index) % 13
            if offset != 0:
                core_matrix[row_index + 1, col_index + 1] = 1.0 if offset in residues else -1.0
    upper_block = np.array([[1.0, 1.0], [1.0, -1.0]])
    diagonal_block = np.array([[1.0, -1.0], [-1.0, -1.0]])
    return np.kron(core_matrix, upper_block) + np.kron(np.eye(14), diagonal_block)


def sylvester(matrix_order):
    positions = jnp.arange(matrix_order, dtype=jnp.int32)
    common_bits = jnp.bitwise_and(positions[:, None], positions[None, :])
    parity = jnp.zeros((matrix_order, matrix_order), jnp.int32)
    for bit_shift in range(matrix_order.bit_length() - 1):
        parity = parity + jnp.bitwise_and(jnp.right_shift(common_bits, bit_shift), 1)
    return (1 - 2 * (parity % 2)).astype(jnp.float32)


def rotate(rows_in, small_table, large_table):
    row_count, width = rows_in.shape
    large_order = large_table.shape[0]
    small_order = small_table.shape[0]
    first_section = jnp.dot(
        rows_in.reshape(row_count * small_order, large_order),
        large_table,
        preferred_element_type=jnp.float32,
    )
    first_section = first_section.reshape(row_count, small_order, large_order)
    rotated = jnp.einsum("ac,tad->tcd", small_table, first_section, precision=lax.Precision.HIGHEST)
    return rotated.reshape(row_count, width) * (1.0 / math.sqrt(width))


def quantize(rotated):
    grouped = rotated.reshape(rotated.shape[0], -1, GROUP)
    largest = jnp.max(jnp.abs(grouped), axis=-1, keepdims=True)
    spacing = largest * (0.9 / 7.0) + 1e-06
    scaled = grouped / spacing
    staircase = jnp.minimum(scaled - jnp.sin(2.0 * math.pi * scaled) / (2.0 * math.pi), 7.0)
    return (staircase * spacing).reshape(rotated.shape).astype(jnp.bfloat16)


def per_device(gate_pre, up_pre, down_weight, out_grad):
    small_table = jnp.asarray(paley_table(), jnp.float32)
    large_table = sylvester(HAD_LARGE).astype(jnp.bfloat16)
    gate_wide = gate_pre.astype(jnp.float32)
    up_wide = up_pre.astype(jnp.float32)
    sigmoid_gate = jax.nn.sigmoid(gate_wide)
    activated = gate_wide * sigmoid_gate
    hidden = (activated * up_wide).astype(jnp.bfloat16)
    full_grad = lax.all_gather(out_grad, "tensor", axis=1, tiled=True)
    rot_grad = lax.dot_general(
        full_grad, down_weight, (((1,), (1,)), ((), ())), preferred_element_type=jnp.float32
    ).astype(jnp.bfloat16)
    token_hidden = lax.all_to_all(hidden, "tensor", split_axis=0, concat_axis=1, tiled=True)
    quant_rows = quantize(rotate(token_hidden, small_table, large_table))
    quantized = lax.all_to_all(quant_rows, "tensor", split_axis=1, concat_axis=0, tiled=True)
    token_grad = lax.all_to_all(rot_grad, "tensor", split_axis=0, concat_axis=1, tiled=True)
    back_rows = rotate(token_grad, small_table.T, large_table.T).astype(jnp.bfloat16)
    hidden_grad = lax.all_to_all(back_rows, "tensor", split_axis=1, concat_axis=0, tiled=True)
    partial_grad = lax.dot_general(
        quantized, full_grad, (((0,), (0,)), ((), ())), preferred_element_type=jnp.float32
    )
    grad_down = lax.psum_scatter(partial_grad, "dp", scatter_dimension=1, tiled=True).astype(
        jnp.bfloat16
    )
    hid_wide = hidden_grad.astype(jnp.float32)
    grad_up = (hid_wide * activated).astype(jnp.bfloat16)
    grad_gate = (
        hid_wide * up_wide * sigmoid_gate * (1.0 + gate_wide * (1.0 - sigmoid_gate))
    ).astype(jnp.bfloat16)
    return (grad_gate, grad_up, grad_down)


def conference():
    signs = paley_table()[::2, ::2].copy()
    np.fill_diagonal(signs, 0.0)
    return signs


SINE = tuple((0.9999999944722885, -6.579735439437039, 12.987842893122675, -12.207428862951517, 6.6870661467168215, -2.3663670610371574, 0.5091905912043592))


def greet(n, sibling=False):
    me = lax.axis_index("tensor")
    barrier = pltpu.get_barrier_semaphore()
    for step in range(1, n):
        pl.semaphore_signal(
            barrier, inc=1, device_id={"tensor": lax.rem(me + step, n)}, device_id_type=MESH
        )
    if sibling:
        other = 1 - lax.axis_index("dp")
        pl.semaphore_signal(barrier, inc=1, device_id={"dp": other}, device_id_type=MESH)
    pl.semaphore_wait(barrier, n if sibling else n - 1)


def round_levels(value):
    largest = jnp.max(jnp.abs(value), axis=-1, keepdims=True)
    spacing = largest * (0.9 / 7.0) + 1e-06
    scaled = value * (1.0 / spacing)
    rest = scaled - jnp.round(scaled)
    square = rest * rest
    wave = jnp.full_like(square, SINE[-1])
    for factor in SINE[-2::-1]:
        wave = wave * square + factor
    return jnp.minimum(scaled - wave * rest, 7.0) * spacing


def exchange_copies(n, chunk, source, target, send, recv):
    me = lax.axis_index("tensor")
    rows = pl.ds(pl.multiple_of(chunk * CHUNK, CHUNK), CHUNK)
    copies = []
    for step in sorted(range(1, n), key=lambda s: abs(s - n // 2)):
        peer = lax.rem(me + step, n)
        copies.append(
            pltpu.make_async_remote_copy(
                src_ref=source.at[peer, rows],
                dst_ref=target.at[me, rows],
                send_sem=send.at[chunk, step],
                recv_sem=recv.at[chunk, step],
                device_id={"tensor": peer},
                device_id_type=MESH,
            )
        )
    local = pltpu.make_async_copy(
        source.at[me, rows], target.at[me, rows], recv.at[chunk, 0]
    )
    return copies, local


def exchange(n, chunk, *refs):
    copies, local = exchange_copies(n, chunk, *refs)
    for copy in copies:
        copy.start()
    local.start()


def arrived(n, chunk, *refs):
    copies, local = exchange_copies(n, chunk, *refs)
    for copy in copies:
        copy.wait_recv()
    local.wait()


def sent(n, chunk, *refs):
    for copy in exchange_copies(n, chunk, *refs)[0]:
        copy.wait_send()


def each_chunk(action, n, *refs):
    @pl.loop(0, refs[0].shape[1] // CHUNK)
    def _(chunk):
        action(n, chunk, *refs)


def gather_columns(n, out_grad, grad_v, sems, meanwhile, between):
    me = lax.axis_index("tensor")
    line = n // 2
    width = out_grad.shape[1]
    row, side = me // 2, lax.rem(me, 2)

    def slot(at_row, at_side):
        place = lax.rem(at_row + line, line) * 2 + at_side
        return grad_v.at[:, pl.ds(pl.multiple_of(place * width, width), width)]

    def push(source_row, peer, at):
        return pltpu.make_async_remote_copy(
            src_ref=slot(source_row, side),
            dst_ref=slot(source_row, side),
            send_sem=sems.at[0, at],
            recv_sem=sems.at[1, at],
            device_id={"tensor": peer},
            device_id_type=MESH,
        )

    def along(sign, hop):
        peer = lax.rem(row + sign + line, line) * 2 + side
        return push(row - sign * (hop - 1), peer, hop if sign > 0 else line + hop)

    def across(sign, hop):
        at = 2 * line + (0 if hop == 0 else hop if sign > 0 else line + hop)
        return push(row - sign * hop, row * 2 + 1 - side, at)

    def has(sign, hop):
        return row - hop >= 0 if sign > 0 else row + hop < line

    for sign in (1, -1):
        pl.when(has(-sign, 1))(lambda sign=sign: along(sign, 1).start())
    across(1, 0).start()
    meanwhile()
    for hop in range(1, line):
        for sign in (1, -1):

            @pl.when(has(sign, hop))
            def _(sign=sign, hop=hop):
                along(sign, hop).wait_recv()
                if hop + 1 < line:
                    pl.when(has(-sign, 1))(lambda: along(sign, hop + 1).start())
                across(sign, hop).start()

        if hop == line // 2:
            between()
    across(1, 0).wait()
    for hop in range(1, line):
        for sign in (1, -1):

            @pl.when(has(sign, hop))
            def _(sign=sign, hop=hop):
                across(sign, hop).wait()

            @pl.when(has(sign, hop - 1) & has(-sign, 1))
            def _(sign=sign, hop=hop):
                along(sign, hop).wait_send()


def rotate_pieces(n, quantized, chunk, in_v, table_v, mid_v, out_v):
    tokens = CHUNK
    per = in_v.shape[2] // PIECE
    scale = 1.0 / math.sqrt(n * per * PIECE)
    rows = pl.ds(pl.multiple_of(chunk * CHUNK, CHUNK), CHUNK)
    stacked = jnp.concatenate(
        [
            in_v[at, rows, PIECE * k : PIECE * (k + 1)]
            for at in range(n)
            for k in range(per)
        ],
        axis=0,
    )
    first = jnp.dot(stacked, table_v[...], preferred_element_type=jnp.float32)
    mid_v[...] = first.reshape(n * per, tokens, PIECE)

    signs = conference()
    order = signs.shape[0]
    lane_tiles = PIECE // GROUP

    @pl.loop(0, lane_tiles)
    def _(step):
        lane = step * GROUP
        lanes = pl.ds(pl.multiple_of(lane, GROUP), GROUP)

        def total(i, j, half):
            even, odd = mid_v[i * 4 + j * 2, :, lanes], mid_v[i * 4 + j * 2 + 1, :, lanes]
            return even - odd if half else even + odd

        for half in range(2):
            mixed = [[None] * order, [None] * order]
            for i in range(order):
                one, two = total(i, 0, half), total(i, 1, half)
                mixed[0][i] = one + two
                mixed[1][i] = one - two
            for j in range(2):
                for i in range(order):
                    value = mixed[1][i] if j == 0 else -mixed[0][i]
                    for other in range(order):
                        if signs[other, i] > 0:
                            value = value + mixed[j][other]
                        elif signs[other, i] < 0:
                            value = value - mixed[j][other]
                    value = value * scale
                    if quantized:
                        value = round_levels(value)
                    unit = i * 4 + j * 2 + half
                    place = pl.ds(pl.multiple_of(lane + unit % per * PIECE, GROUP), GROUP)
                    out_v[unit // per, rows, place] = value.astype(out_v.dtype)


def whole_kernel(
    n, gate, up, out_grad, weight, table, hidden_grad, grad_down,
    hidden_v, token_v, rot_v, back_in_v, mid_v, out_v, back_v, quant_v,
    grad_v, side_grad_v, weight_v, down_v, table_v,
    gather_sem, send, recv, side_send, side_recv, local_sem, weight_sem, down_sem,
):
    me = lax.axis_index("tensor")
    core = lax.axis_index("dp")
    tokens, width = out_grad.shape
    part = tokens // n
    features = n * width
    half = features // 2
    tiles = weight.shape[0] // 256
    mine = pl.ds(pl.multiple_of(me * width, width), width)
    loads = [
        pltpu.make_async_copy(source, target, local_sem.at[at])
        for at, (source, target) in enumerate(
            [(gate, out_v), (up, back_v), (table, table_v), (out_grad, grad_v.at[:, mine])]
        )
    ]
    for copy in loads:
        copy.start()

    def fetch(tile):
        slot = lax.rem(tile, 2)
        rows = pl.ds(pl.multiple_of(tile * 256, 256), 256)
        return pltpu.make_async_copy(weight.at[rows], weight_v.at[slot], weight_sem.at[slot])

    fetch(0).start()
    greet(n, sibling=True)
    loads[3].wait()

    to_tokens, grads_to_tokens, levels, grads_back = [
        (source, target, send.at[at], recv.at[at])
        for at, (source, target) in enumerate(
            [
                (hidden_v, token_v),
                (rot_v, back_in_v),
                (out_v, quant_v.at[pl.ds(0, n)]),
                (back_v, hidden_grad),
            ]
        )
    ]

    def make_hidden():
        loads[0].wait()
        loads[1].wait()

        @pl.loop(0, n * part // 16)
        def _(step):
            at = step // (part // 16)
            rows = pl.ds(pl.multiple_of(step % (part // 16) * 16, 16), 16)
            wide = out_v[at, rows, :].astype(jnp.float32)
            active = wide * jax.nn.sigmoid(wide)
            hidden_v[at, rows, :] = (active * back_v[at, rows, :].astype(jnp.float32)).astype(
                hidden_v.dtype
            )

    def send_hidden():
        each_chunk(exchange, n, *to_tokens)

    gather_columns(n, out_grad, grad_v, gather_sem, make_hidden, send_hidden)


    def beside(which):
        return grad_v.at[:, pl.ds(pl.multiple_of(which * half, half), half)]

    def to_sibling(source, target, at):
        copy = pltpu.make_async_remote_copy(
            src_ref=source,
            dst_ref=target,
            send_sem=side_send.at[at],
            recv_sem=side_recv.at[at],
            device_id={"dp": 1 - core},
            device_id_type=MESH,
        )
        copy.start()
        return copy

    side_grad = to_sibling(beside(1 - core), side_grad_v, 0)
    loads[2].wait()

    @pl.loop(0, part // CHUNK)
    def _(chunk):
        arrived(n, chunk, *to_tokens)
        rotate_pieces(n, True, chunk, token_v, table_v, mid_v, out_v)
        exchange(n, chunk, *levels)

    @pl.loop(0, tiles)
    def _(tile):
        pl.when(tile + 1 < tiles)(lambda: fetch(tile + 1).start())
        fetch(tile).wait()
        units = pl.ds(pl.multiple_of(tile * 256, 256), 256)
        product = lax.dot_general(
            grad_v[...], weight_v[lax.rem(tile, 2)], (((1,), (1,)), ((), ())),
            preferred_element_type=jnp.float32,
        )
        rot_v[:, :, units] = product.astype(rot_v.dtype).reshape(n, part, 256)

    each_chunk(exchange, n, *grads_to_tokens)

    @pl.loop(0, part // CHUNK)
    def _(chunk):
        arrived(n, chunk, *grads_to_tokens)
        rotate_pieces(n, False, chunk, back_in_v, table_v, mid_v, back_v)
        exchange(n, chunk, *grads_back)

    each_chunk(arrived, n, *levels)
    side_levels = to_sibling(quant_v.at[pl.ds(0, n)], quant_v.at[pl.ds(n, n)], 1)
    side_grad.wait()
    side_levels.wait()

    def write(tile):
        slot = lax.rem(tile, 2)
        rows = pl.ds(pl.multiple_of(tile * 256, 256), 256)
        return pltpu.make_async_copy(down_v.at[slot], grad_down.at[rows], down_sem.at[slot])

    own_columns = pl.ds(pl.multiple_of(core * half, half), half)

    @pl.loop(0, tiles)
    def _(tile):
        pl.when(tile >= 2)(lambda: write(tile - 2).wait())
        units = pl.ds(pl.multiple_of(tile * 256, 256), 256)
        rows = quant_v[:, :, units].reshape(2, tokens, 256)
        total = jnp.dot(rows[0].T, grad_v[:, own_columns], preferred_element_type=jnp.float32)
        total += jnp.dot(rows[1].T, side_grad_v[...], preferred_element_type=jnp.float32)
        down_v[lax.rem(tile, 2)] = total.astype(down_v.dtype)
        write(tile).start()

    for tile in range(max(tiles - 2, 0), tiles):
        write(tile).wait()
    each_chunk(arrived, n, *grads_back)
    for refs in (to_tokens, grads_to_tokens, levels, grads_back):
        each_chunk(sent, n, *refs)


def with_kernel(n, gate_pre, up_pre, down_weight, out_grad):
    tokens, units = gate_pre.shape
    width, part = out_grad.shape[1], tokens // n
    features = n * width
    blocks = (n, part, units)
    wide = jnp.bfloat16
    table = jnp.asarray(functools.reduce(np.kron, [[[1.0, 1.0], [1.0, -1.0]]] * (PIECE.bit_length() - 1)), wide)
    dma = pltpu.SemaphoreType.DMA
    keep = pltpu.VMEM(blocks, wide)
    hidden_grad, grad_down = pl.pallas_call(
        functools.partial(whole_kernel, n),
        out_shape=[
            jax.ShapeDtypeStruct(blocks, wide),
            jax.ShapeDtypeStruct((units, features // 2), wide),
        ],
        in_specs=[ANY] * 5,
        out_specs=[ANY] * 2,
        scratch_shapes=[
            keep, keep, keep, keep,
            pltpu.VMEM((n * units // PIECE, CHUNK, PIECE), jnp.float32),
            keep, keep,
            pltpu.VMEM((2 * n, part, units), wide),
            pltpu.VMEM((tokens, features), wide),
            pltpu.VMEM((tokens, features // 2), wide),
            pltpu.VMEM((2, 256, features), wide),
            pltpu.VMEM((2, 256, features // 2), wide),
            pltpu.VMEM((PIECE, PIECE), wide),
            dma((2, 2 * n)), dma((4, part // CHUNK, n)), dma((4, part // CHUNK, n)), dma((2,)), dma((2,)),
            dma((4,)), dma((2,)), dma((2,)),
        ],
        compiler_params=pltpu.CompilerParams(
            collective_id=1, has_side_effects=True, vmem_limit_bytes=VMEM_LIMIT
        ),
        cost_estimate=pl.CostEstimate(
            flops=4 * tokens * units * features, bytes_accessed=60_000_000, transcendentals=0
        ),
    )(gate_pre.reshape(blocks), up_pre.reshape(blocks), out_grad, down_weight, table)
    gate_wide = gate_pre.astype(jnp.float32)
    up_wide = up_pre.astype(jnp.float32)
    sigmoid_gate = jax.nn.sigmoid(gate_wide)
    activated = gate_wide * sigmoid_gate
    hid_wide = hidden_grad.reshape(tokens, units).astype(jnp.float32)
    grad_up = (hid_wide * activated).astype(wide)
    grad_gate = (
        hid_wide * up_wide * sigmoid_gate * (1.0 + gate_wide * (1.0 - sigmoid_gate))
    ).astype(wide)
    return (grad_gate, grad_up, grad_down)


def choose(n, cores, gate_pre, up_pre, down_weight, out_grad):
    tokens, units = gate_pre.shape
    fits = (
        n % 2 == 0 and 4 <= n <= 16 and cores == 2
        and tokens % (CHUNK * n) == 0 and units % PIECE == 0 and units % 256 == 0
        and n * units == 28 * HAD_LARGE and out_grad.shape[1] % 128 == 0
    )
    if fits:
        return with_kernel(n, gate_pre, up_pre, down_weight, out_grad)
    return per_device(gate_pre, up_pre, down_weight, out_grad)


def solution(mesh):
    return jax.shard_map(
        functools.partial(choose, mesh.shape["tensor"], mesh.shape["dp"]),
        mesh=mesh,
        in_specs=(
            P(("groups", "dp"), "tensor"),
            P(("groups", "dp"), "tensor"),
            P("tensor", None),
            P(("groups", "dp"), "tensor"),
        ),
        out_specs=(
            P(("groups", "dp"), "tensor"),
            P(("groups", "dp"), "tensor"),
            P(("groups", "tensor"), "dp"),
        ),
        check_vma=False,
    )
```
